32 devices in a mesh: groups: 2 (over y), row: 4 (over z), col: 4 (over x, core).
Axes of the slice: x: 2, y: 2, z: 4, core: 2. Of those that a mesh axis runs over, the one named last changes fastest.
Arguments:
- tokens: bfloat16 [128, 8192], P(('groups', 'row'), 'col'), parts along dimension 0, may hold values from -6 to 6
- gate_weight: bfloat16 [8192, 26624], P('col', 'row'), may hold values from -0.0625 to 0.0625
- up_weight: bfloat16 [8192, 26624], P('col', 'row'), may hold values from -0.0625 to 0.0625
- down_weight: bfloat16 [26624, 8192], P('row', 'col'), may hold values from -0.0390625 to 0.0390625
Outputs:
- mixed: bfloat16 [128, 8192], P(('groups', 'row'), 'col'), parts along dimension 0
The draws below stay inside these ranges and needn't reach their ends.
There are 2 independent parts, one for each index of `groups`. The reference program is written for one: setup_inputs(seed, part) draws one part's arguments, and reference() takes and returns one part's arrays. A program takes and returns all parts, laid end to end along the dimension named above; an argument that names none is the same for every part. Nothing has to cross between parts.
All inputs are finite; a program needn't handle non-finite values.
Results may differ from the reference program's by a relative error of at most 0.019.
Values may be sent and summed in bfloat16 or wider, within the bound.
A program may use at most 192 MiB of HBM per device.

```python
import jax
import jax.numpy as jnp
from jax import lax

D = 8192
FF = 26624
TOKENS = 64
N_COL = 4


def level_of(stream_key, extent, shards, low, high):
    factor_of, own = 1.0, jax.random.fold_in(stream_key, 6)
    for position, shards_of in shards:
        draws = jnp.exp(jax.random.uniform(jax.random.fold_in(own, position), (shards_of,), jnp.float32, low / len(shards), high / len(shards)))
        factor_of = factor_of * jnp.repeat(draws, extent[position] // shards_of).reshape([-1 if axis == position else 1 for axis in range(len(extent))])
    return factor_of


def centred(stream_key, shape, deviation, limit, pieces=(), dtype=jnp.bfloat16):
    result = deviation * jax.random.normal(stream_key, shape, jnp.float32)
    if pieces:
        result = result * level_of(stream_key, shape, pieces, -0.22, 0.18)
    return jnp.clip(result, -limit, limit).astype(dtype)


def setup_inputs(seed: int = 0, part: int = 0) -> dict:
    seeds = jax.random.split(jax.random.key(seed), 5)
    part_splits = jax.random.split(jax.random.fold_in(seeds[4], part), 5)
    tokens = centred(part_splits[0], (TOKENS, D), 1.0, 6.0, ((0, 4), (1, 4)))
    gate_weight = centred(seeds[1], (D, FF), D ** -0.5, 0.0625, ((0, 4), (1, 4)))
    up_weight = centred(seeds[2], (D, FF), D ** -0.5, 0.0625, ((0, 4), (1, 4)))
    down_weight = centred(seeds[3], (FF, D), FF ** -0.5, 0.0390625, ((0, 4), (1, 4)))
    return dict(tokens=tokens, gate_weight=gate_weight, up_weight=up_weight, down_weight=down_weight)


def reference(tokens, gate_weight, up_weight, down_weight):
    slab_width = D // N_COL
    total_rows = tokens.shape[0]

    def accumulate(segment, totals):
        offset = segment.astype(jnp.int32) * slab_width
        picked = lax.dynamic_slice_in_dim(tokens, offset, slab_width, 1)
        gate_slab = lax.dynamic_slice_in_dim(gate_weight, offset, slab_width, 0)
        up_slab = lax.dynamic_slice_in_dim(up_weight, offset, slab_width, 0)
        gate_part = jnp.dot(picked, gate_slab, preferred_element_type=jnp.float32).astype(jnp.bfloat16)
        up_part = jnp.dot(picked, up_slab, preferred_element_type=jnp.float32).astype(jnp.bfloat16)
        gate_part, up_part = lax.optimization_barrier((gate_part, up_part))
        return (totals[0] + gate_part.astype(jnp.float32), totals[1] + up_part.astype(jnp.float32))

    start_sums = (jnp.zeros((total_rows, FF), jnp.float32), jnp.zeros((total_rows, FF), jnp.float32))
    gate, up = lax.fori_loop(0, N_COL, accumulate, start_sums)
    hidden = (jax.nn.silu(gate) * up).astype(jnp.bfloat16)
    return jnp.dot(hidden, down_weight, preferred_element_type=jnp.float32).astype(jnp.bfloat16)
```

```python
import functools

import jax
import jax.numpy as jnp
from jax import lax
from jax.experimental import pallas as pl
from jax.experimental.pallas import tpu as pltpu
from jax.sharding import PartitionSpec as P

MESH = pl.DeviceIdType.MESH
WIDTH = 256


def swiglu(gate, up):
    return (jax.nn.silu(gate) * up).astype(jnp.bfloat16)


def plain(tokens, gate_weight, up_weight, down_weight):
    local_width = gate_weight.shape[1]
    portion = lax.all_gather(tokens, "row", axis=0, tiled=True)
    gate_part = jnp.dot(portion, gate_weight, preferred_element_type=jnp.float32)
    up_part = jnp.dot(portion, up_weight, preferred_element_type=jnp.float32)
    partials = jnp.concatenate([gate_part, up_part], axis=1)
    summed = lax.psum(partials.astype(jnp.bfloat16), "col").astype(jnp.float32)
    hidden = swiglu(summed[:, :local_width], summed[:, local_width:])
    return lax.psum_scatter(
        jnp.dot(hidden, down_weight, preferred_element_type=jnp.float32).astype(jnp.bfloat16),
        "row",
        scatter_dimension=0,
        tiled=True,
    )


def kernel(
    tok_hbm, gate_hbm, up_hbm, down_hbm, out_ref,
    tok, gate_v, up_v, down_v, pown, cs, cr, sown, xs, xr, hid, acc, obuf, zr, ys, yr,
    own_sem, gate_sem, up_sem, down_sem,
    tz_send, tz_recv, ty_send, ty_recv,
    c_send, c_recv, x_send, x_recv, hx_send, hx_recv, hy_send, hy_recv, hz_send, hz_recv,
    h0_send, h0_recv, h1_send, h1_recv, oz_send, oz_recv, oy_send, oy_recv,
):
    g, r, c = lax.axis_index("groups"), lax.axis_index("row"), lax.axis_index("col")
    x, core = c // 2, c % 2
    core_peer = {"col": x * 2 + (1 - core)}
    x_peer = {"col": (1 - x) * 2 + core}
    y_peer = {"groups": 1 - g}
    others = [(r + k) % 4 for k in (1, 2, 3)]
    b = tok_hbm.shape[0]
    chunks = gate_v.shape[0]
    half = chunks * WIDTH
    out_half = down_v.shape[3]
    T = 8 * b
    q, h = T // 4, T // 2

    def place(group, row):
        return ((group + core) % 2) * 4 + ((row // 2 + x) % 2) * 2 + row % 2

    def slot(group, row):
        return tok.at[place(group, row)]

    barrier = pltpu.get_barrier_semaphore()
    for peer in [core_peer, x_peer, y_peer] + [{"row": o} for o in others]:
        pl.semaphore_signal(barrier, inc=1, device_id=peer, device_id_type=MESH)

    own = pltpu.make_async_copy(tok_hbm, slot(g, r), own_sem)
    own.start()

    def gate_copy(i):
        at = pl.ds(pl.multiple_of(g * half + i * WIDTH, WIDTH), WIDTH)
        return pltpu.make_async_copy(gate_hbm.at[:, at], gate_v.at[i], gate_sem.at[i])

    def up_copy(i):
        at = pl.ds(pl.multiple_of(g * half + i * WIDTH, WIDTH), WIDTH)
        return pltpu.make_async_copy(up_hbm.at[:, at], up_v.at[i], up_sem.at[i])

    def down_copy(side, i):
        source = (g + side) % 2
        rows = pl.ds(pl.multiple_of(source * half + i * WIDTH, WIDTH), WIDTH)
        columns = pl.ds(pl.multiple_of(g * out_half, 128), out_half)
        return pltpu.make_async_copy(down_hbm.at[rows, columns], down_v.at[side, i], down_sem.at[side, i])

    gate_copy(0).start()
    up_copy(0).start()
    pl.semaphore_wait(barrier, 6)

    def send(src, dst, send_sem, recv_sem, peer):
        return pltpu.make_async_remote_copy(
            src_ref=src, dst_ref=dst, send_sem=send_sem, recv_sem=recv_sem,
            device_id=peer, device_id_type=MESH,
        )

    def tok_z(k):
        return send(tok_hbm, slot(g, r), tz_send.at[k - 1], tz_recv.at[k - 1], {"row": (r + k) % 4})

    def tok_z_in(k):
        block = slot(g, (r + 4 - k) % 4)
        return send(block, block, tz_send.at[k - 1], tz_recv.at[k - 1], {"row": (r + k) % 4})

    def tok_y(k):
        block = slot(g, (r + 4 - k) % 4)
        return send(tok_hbm if k == 0 else block, block, ty_send.at[k], ty_recv.at[k], y_peer)

    def tok_y_in(k):
        block = slot(1 - g, (r + 4 - k) % 4)
        return send(block, block, ty_send.at[k], ty_recv.at[k], y_peer)

    for k in (2, 1, 3):
        tok_z(k).start()
    tok_y(0).start()

    def start_weights(i, carry):
        gate_copy(i).start()
        up_copy(i).start()
        return carry

    def start_down(i, carry):
        down_copy(0, i).start()
        down_copy(1, i).start()
        return carry

    lax.fori_loop(1, chunks, start_weights, 0)
    lax.fori_loop(0, chunks, start_down, 0)

    for k in (1, 3, 2):
        tok_z_in(k).wait_recv()
        tok_y(k).start()
    own.wait()
    for k in (0, 1, 3, 2):
        tok_y_in(k).wait_recv()

    acc[...] = jnp.zeros_like(acc)

    def c_copy(i):
        return send(cs.at[i], cr.at[i], c_send.at[i], c_recv.at[i], core_peer)

    def x_copy(i):
        return send(xs.at[i], xr.at[i], x_send.at[i], x_recv.at[i], x_peer)

    def hx_copy(i):
        return send(hid.at[0, i, pl.ds(0, q)], hid.at[0, i, pl.ds(q, q)], hx_send.at[i], hx_recv.at[i], x_peer)

    def hy_copy(i):
        return send(hid.at[0, i, pl.ds(0, q)], hid.at[1, i, pl.ds(0, q)], hy_send.at[i], hy_recv.at[i], y_peer)

    def hz_copy(i):
        return send(hid.at[0, i, pl.ds(q, q)], hid.at[1, i, pl.ds(q, q)], hz_send.at[i], hz_recv.at[i], y_peer)

    def h0_copy(i):
        return send(hid.at[0, i, pl.ds(0, h)], hid.at[0, i, pl.ds(h, h)], h0_send.at[i], h0_recv.at[i], core_peer)

    def h1_copy(i):
        return send(hid.at[1, i, pl.ds(0, h)], hid.at[1, i, pl.ds(h, h)], h1_send.at[i], h1_recv.at[i], core_peer)

    def project(i):
        gate_copy(i).wait()
        up_copy(i).wait()
        t = tok[...].reshape(T, tok.shape[2])
        for side, w in enumerate((gate_v, up_v)):
            p = jnp.dot(t, w[i], preferred_element_type=jnp.float32)
            at = slice(side * WIDTH, (side + 1) * WIDTH)
            pown[i, :, at] = p[:h]
            cs[i, :, at] = p[h:].astype(jnp.bfloat16)
        c_copy(i).start()

    def add_core(i):
        c_copy(i).wait_recv()
        s = pown[i] + cr[i].astype(jnp.float32)
        sown[i] = s[:q]
        xs[i] = s[q:].astype(jnp.bfloat16)
        x_copy(i).start()

    def add_x(i):
        x_copy(i).wait_recv()
        s = sown[i] + xr[i].astype(jnp.float32)
        gate, up = s[:, :WIDTH], s[:, WIDTH:]
        hid[0, i, pl.ds(0, q), :] = (gate / (1.0 + jnp.exp(-gate)) * up).astype(jnp.bfloat16)
        hx_copy(i).start()
        hy_copy(i).start()

    def spread(i):
        hx_copy(i).wait_recv()
        hz_copy(i).start()
        h0_copy(i).start()

    def spread_y(i):
        hy_copy(i).wait_recv()
        hz_copy(i).wait_recv()
        h1_copy(i).start()

    def contract(i):
        down_copy(0, i).wait()
        down_copy(1, i).wait()
        h0_copy(i).wait_recv()
        h1_copy(i).wait_recv()
        acc[...] += jnp.dot(hid[0, i], down_v[0, i], preferred_element_type=jnp.float32) + jnp.dot(
            hid[1, i], down_v[1, i], preferred_element_type=jnp.float32
        )

    stages = ((spread_y, 5), (spread, 4), (add_x, 2), (add_core, 1), (project, 0), (contract, 6))
    depth = 6

    def step(t, carry):
        for stage, lag in stages:
            i = t - lag
            pl.when(jnp.logical_and(i >= 0, i < chunks))(functools.partial(stage, i))
        return carry

    lax.fori_loop(0, chunks + depth, step, 0)

    def oz_copy(k):
        row = (r + k) % 4
        at = ((row // 2 + x) % 2) * 2 + row % 2
        return send(obuf.at[:, at], zr.at[k - 1], oz_send.at[k - 1], oz_recv.at[k - 1], {"row": row})

    obuf[...] = acc[...].astype(jnp.bfloat16).reshape(obuf.shape)
    for k in (2, 1, 3):
        oz_copy(k).start()

    def drain(i, carry):
        for copy in (c_copy, x_copy, hx_copy, hy_copy, hz_copy, h0_copy, h1_copy):
            copy(i).wait_send()
        return carry

    lax.fori_loop(0, chunks, drain, 0)
    for k in (1, 2, 3):
        tok_z(k).wait_send()
    for k in (0, 1, 2, 3):
        tok_y(k).wait_send()

    mine = (r // 2 + x) % 2 * 2 + r % 2
    theirs_at, ours_at = (1 - g + core) % 2, (g + core) % 2

    def rows_of(at):
        first = pl.multiple_of((at * 4 + mine) * b, b)
        return acc[pl.ds(first, b), :]

    for k in (1, 3, 2):
        oz_copy(k).wait_recv()

    def total(at):
        s = rows_of(at)
        for k in range(3):
            s = s + zr[k, at].astype(jnp.float32)
        return s.astype(jnp.bfloat16)

    oy = send(ys, yr, oy_send, oy_recv, y_peer)
    ys[...] = total(theirs_at)
    oy.start()
    out_ref[:, pl.ds(pl.multiple_of(g * out_half, 128), out_half)] = total(ours_at)
    for k in (1, 2, 3):
        oz_copy(k).wait_send()
    oy.wait()
    out_ref[:, pl.ds(pl.multiple_of((1 - g) * out_half, 128), out_half)] = yr[...]


def fused(tokens, gate_weight, up_weight, down_weight):
    b, k = tokens.shape
    units = gate_weight.shape[1]
    n = down_weight.shape[1]
    chunks = units // 2 // WIDTH
    T = 8 * b
    q, h = T // 4, T // 2
    bf16, f32 = jnp.bfloat16, jnp.float32
    dma = pltpu.SemaphoreType.DMA
    per_chunk = dma((chunks,))
    return pl.pallas_call(
        kernel,
        out_shape=jax.ShapeDtypeStruct((b, n), bf16),
        in_specs=[pl.BlockSpec(memory_space=pl.ANY)] * 4,
        out_specs=pl.BlockSpec(memory_space=pltpu.VMEM),
        scratch_shapes=[
            pltpu.VMEM((8, b, k), bf16),
            pltpu.VMEM((chunks, k, WIDTH), bf16),
            pltpu.VMEM((chunks, k, WIDTH), bf16),
            pltpu.VMEM((2, chunks, WIDTH, n // 2), bf16),
            pltpu.VMEM((chunks, h, 2 * WIDTH), f32),
            pltpu.VMEM((chunks, h, 2 * WIDTH), bf16),
            pltpu.VMEM((chunks, h, 2 * WIDTH), bf16),
            pltpu.VMEM((chunks, q, 2 * WIDTH), f32),
            pltpu.VMEM((chunks, q, 2 * WIDTH), bf16),
            pltpu.VMEM((chunks, q, 2 * WIDTH), bf16),
            pltpu.VMEM((2, chunks, T, WIDTH), bf16),
            pltpu.VMEM((T, n // 2), f32),
            pltpu.VMEM((2, 4, b, n // 2), bf16),
            pltpu.VMEM((3, 2, b, n // 2), bf16),
            pltpu.VMEM((b, n // 2), bf16),
            pltpu.VMEM((b, n // 2), bf16),
            dma,
            per_chunk,
            per_chunk,
            dma((2, chunks)),
            dma((3,)),
            dma((3,)),
            dma((4,)),
            dma((4,)),
        ]
        + [per_chunk] * 14
        + [dma((3,)), dma((3,)), dma, dma],
        compiler_params=pltpu.CompilerParams(
            collective_id=0, has_side_effects=True, vmem_limit_bytes=60 * 2**20
        ),
        cost_estimate=pl.CostEstimate(
            flops=3 * T * k * units, bytes_accessed=3 * k * units, transcendentals=q * units // 2
        ),
    )(tokens, gate_weight, up_weight, down_weight)


def fits(mesh, tokens, gate_weight, down_weight):
    s = mesh.shape
    if (s["groups"], s["row"], s["col"]) != (2, 4, 4):
        return False
    b, k = tokens.shape[0] // 8, tokens.shape[1] // 4
    units, n = gate_weight.shape[1] // 4, down_weight.shape[1] // 4
    small = 3 * k * units + 26 * b * units + 24 * b * (k + n)
    return b % 16 == 0 and k % 128 == 0 and units % (2 * WIDTH) == 0 and n % 256 == 0 and small < 56 * 2**20


def solution(mesh):
    specs = dict(
        mesh=mesh,
        in_specs=(P(("groups", "row"), "col"), P("col", "row"), P("col", "row"), P("row", "col")),
        out_specs=P(("groups", "row"), "col"),
        check_vma=False,
    )

    def layer(tokens, gate_weight, up_weight, down_weight):
        body = fused if fits(mesh, tokens, gate_weight, down_weight) else plain
        return jax.shard_map(body, **specs)(tokens, gate_weight, up_weight, down_weight)

    return layer
```

```python
import functools

import jax
import jax.numpy as jnp
from jax import lax
from jax.experimental import pallas as pl
from jax.experimental.pallas import tpu as pltpu
from jax.sharding import PartitionSpec as P

MESH = pl.DeviceIdType.MESH
WIDTH = 256
SLOTS = 11


def swiglu(gate, up):
    return (jax.nn.silu(gate) * up).astype(jnp.bfloat16)


def plain(tokens, gate_weight, up_weight, down_weight):
    local_width = gate_weight.shape[1]
    portion = lax.all_gather(tokens, "row", axis=0, tiled=True)
    gate_part = jnp.dot(portion, gate_weight, preferred_element_type=jnp.float32)
    up_part = jnp.dot(portion, up_weight, preferred_element_type=jnp.float32)
    partials = jnp.concatenate([gate_part, up_part], axis=1)
    summed = lax.psum(partials.astype(jnp.bfloat16), "col").astype(jnp.float32)
    hidden = swiglu(summed[:, :local_width], summed[:, local_width:])
    return lax.psum_scatter(
        jnp.dot(hidden, down_weight, preferred_element_type=jnp.float32).astype(jnp.bfloat16),
        "row",
        scatter_dimension=0,
        tiled=True,
    )


def kernel(
    tok_hbm, gate_hbm, up_hbm, down_hbm, out_ref,
    tok, gate_v, up_v, down_v, pown, cs, cr, sown, xs, xr, hid, acc, obuf, zr,
    own_sem, gate_sem, up_sem, down_sem, tz_send, tz_recv,
    c_send, c_recv, x_send, x_recv, hx_send, hx_recv, h0_send, h0_recv, oz_send, oz_recv,
):
    g, r, c = lax.axis_index("groups"), lax.axis_index("row"), lax.axis_index("col")
    x, core = c // 2, c % 2
    core_peer = {"col": x * 2 + (1 - core)}
    x_peer = {"col": (1 - x) * 2 + core}
    b = tok_hbm.shape[0]
    slots = gate_v.shape[0]
    chunks = down_v.shape[0]
    T = 4 * b
    q, h = b, 2 * b

    def place(row):
        return ((row // 2 + core) % 2) * 2 + (row % 2 + x) % 2

    barrier = pltpu.get_barrier_semaphore()
    for peer in [core_peer, x_peer] + [{"row": (r + k) % 4} for k in (1, 2, 3)]:
        pl.semaphore_signal(barrier, inc=1, device_id=peer, device_id_type=MESH)

    own = pltpu.make_async_copy(tok_hbm, tok.at[place(r)], own_sem)
    own.start()

    def gate_copy(i):
        at = pl.ds(pl.multiple_of(i * WIDTH, WIDTH), WIDTH)
        return pltpu.make_async_copy(gate_hbm.at[:, at], gate_v.at[i % slots], gate_sem.at[i % slots])

    def up_copy(i):
        at = pl.ds(pl.multiple_of(i * WIDTH, WIDTH), WIDTH)
        return pltpu.make_async_copy(up_hbm.at[:, at], up_v.at[i % slots], up_sem.at[i % slots])

    def down_copy(i):
        rows = pl.ds(pl.multiple_of(i * WIDTH, WIDTH), WIDTH)
        return pltpu.make_async_copy(down_hbm.at[rows], down_v.at[i], down_sem.at[i])

    def start_weights(i, carry):
        gate_copy(i).start()
        up_copy(i).start()
        return carry

    def start_down(i, carry):
        down_copy(i).start()
        return carry

    start_weights(0, 0)
    pl.semaphore_wait(barrier, 5)

    def send(src, dst, send_sem, recv_sem, peer):
        return pltpu.make_async_remote_copy(
            src_ref=src, dst_ref=dst, send_sem=send_sem, recv_sem=recv_sem,
            device_id=peer, device_id_type=MESH,
        )

    def tok_copy(k):
        to = {"row": (r + k) % 4}
        return send(tok_hbm, tok.at[place(r)], tz_send.at[k - 1], tz_recv.at[k - 1], to)

    def tok_in(k):
        block = tok.at[place((r + 4 - k) % 4)]
        return send(block, block, tz_send.at[k - 1], tz_recv.at[k - 1], {"row": (r + k) % 4})

    for k in (2, 1, 3):
        tok_copy(k).start()
    lax.fori_loop(1, slots, start_weights, 0)
    acc[...] = jnp.zeros_like(acc)
    own.wait()
    for k in (1, 3, 2):
        tok_in(k).wait_recv()

    def c_copy(i):
        return send(cs.at[i], cr.at[i], c_send.at[i], c_recv.at[i], core_peer)

    def x_copy(i):
        return send(xs.at[i], xr.at[i], x_send.at[i], x_recv.at[i], x_peer)

    def hx_copy(i):
        return send(hid.at[i, pl.ds(0, q)], hid.at[i, pl.ds(q, q)], hx_send.at[i], hx_recv.at[i], x_peer)

    def h0_copy(i):
        return send(hid.at[i, pl.ds(0, h)], hid.at[i, pl.ds(h, h)], h0_send.at[i], h0_recv.at[i], core_peer)

    def project(i):
        gate_copy(i).wait()
        up_copy(i).wait()
        t = tok[...].reshape(T, tok.shape[2])
        for side, w in enumerate((gate_v, up_v)):
            p = jnp.dot(t, w[i % slots], preferred_element_type=jnp.float32)
            at = slice(side * WIDTH, (side + 1) * WIDTH)
            pown[i, :, at] = p[:h]
            cs[i, :, at] = p[h:].astype(jnp.bfloat16)
        c_copy(i).start()

        @pl.when(i + slots < chunks)
        def _():
            start_weights(i + slots, 0)

        @pl.when(i == max(chunks - slots - 1, 0))
        def _():
            lax.fori_loop(0, chunks, start_down, 0)

    def add_core(i):
        c_copy(i).wait_recv()
        s = pown[i] + cr[i].astype(jnp.float32)
        sown[i] = s[:q]
        xs[i] = s[q:].astype(jnp.bfloat16)
        x_copy(i).start()

    def add_x(i):
        x_copy(i).wait_recv()
        s = sown[i] + xr[i].astype(jnp.float32)
        gate, up = s[:, :WIDTH], s[:, WIDTH:]
        hid[i, pl.ds(0, q), :] = (gate / (1.0 + jnp.exp(-gate)) * up).astype(jnp.bfloat16)
        hx_copy(i).start()

    def spread(i):
        hx_copy(i).wait_recv()
        h0_copy(i).start()

    def contract(i):
        down_copy(i).wait()
        h0_copy(i).wait_recv()
        acc[...] += jnp.dot(hid[i], down_v[i], preferred_element_type=jnp.float32)

    stages = ((spread, 18), (add_x, 10), (add_core, 2), (project, 0), (contract, 20))

    def step(t, carry):
        for stage, lag in stages:
            i = t - lag
            pl.when(jnp.logical_and(i >= 0, i < chunks))(functools.partial(stage, i))
        return carry

    lax.fori_loop(0, chunks + 20, step, 0)

    def out_copy(k):
        row = (r + k) % 4
        return send(obuf.at[place(row)], zr.at[k - 1], oz_send.at[k - 1], oz_recv.at[k - 1], {"row": row})

    obuf[...] = acc[...].astype(jnp.bfloat16).reshape(obuf.shape)
    for k in (2, 1, 3):
        out_copy(k).start()

    def drain(i, carry):
        for copy in (c_copy, x_copy, hx_copy, h0_copy):
            copy(i).wait_send()
        return carry

    lax.fori_loop(0, chunks, drain, 0)
    for k in (1, 2, 3):
        tok_copy(k).wait_send()
    total = acc[pl.ds(pl.multiple_of(place(r) * b, b), b), :]
    for k in (1, 3, 2):
        out_copy(k).wait_recv()
        total = total + zr[k - 1].astype(jnp.float32)
    out_ref[...] = total.astype(jnp.bfloat16)
    for k in (1, 2, 3):
        out_copy(k).wait_send()


def fused(tokens, gate_weight, up_weight, down_weight):
    b, k = tokens.shape
    units = gate_weight.shape[1]
    n = down_weight.shape[1]
    chunks = units // WIDTH
    slots = min(SLOTS, chunks)
    T = 4 * b
    q, h = b, 2 * b
    bf16, f32 = jnp.bfloat16, jnp.float32
    dma = pltpu.SemaphoreType.DMA
    per_chunk = dma((chunks,))
    return pl.pallas_call(
        kernel,
        out_shape=jax.ShapeDtypeStruct((b, n), bf16),
        in_specs=[pl.BlockSpec(memory_space=pl.ANY)] * 4,
        out_specs=pl.BlockSpec(memory_space=pltpu.VMEM),
        scratch_shapes=[
            pltpu.VMEM((4, b, k), bf16),
            pltpu.VMEM((slots, k, WIDTH), bf16),
            pltpu.VMEM((slots, k, WIDTH), bf16),
            pltpu.VMEM((chunks, WIDTH, n), bf16),
            pltpu.VMEM((chunks, h, 2 * WIDTH), f32),
            pltpu.VMEM((chunks, h, 2 * WIDTH), bf16),
            pltpu.VMEM((chunks, h, 2 * WIDTH), bf16),
            pltpu.VMEM((chunks, q, 2 * WIDTH), f32),
            pltpu.VMEM((chunks, q, 2 * WIDTH), bf16),
            pltpu.VMEM((chunks, q, 2 * WIDTH), bf16),
            pltpu.VMEM((chunks, T, WIDTH), bf16),
            pltpu.VMEM((T, n), f32),
            pltpu.VMEM((4, b, n), bf16),
            pltpu.VMEM((3, b, n), bf16),
            dma,
            dma((slots,)),
            dma((slots,)),
            per_chunk,
            dma((3,)),
            dma((3,)),
        ]
        + [per_chunk] * 8
        + [dma((3,)), dma((3,))],
        compiler_params=pltpu.CompilerParams(
            collective_id=0, has_side_effects=True, vmem_limit_bytes=60 * 2**20
        ),
        cost_estimate=pl.CostEstimate(
            flops=6 * T * k * units, bytes_accessed=6 * k * units, transcendentals=q * units
        ),
    )(tokens, gate_weight, up_weight, down_weight)


def fits(mesh, tokens, gate_weight, down_weight):
    s = mesh.shape
    if (s["groups"], s["row"], s["col"]) != (2, 4, 4):
        return False
    b, k = tokens.shape[0] // 8, tokens.shape[1] // 4
    units, n = gate_weight.shape[1] // 4, down_weight.shape[1] // 4
    held = 4 * SLOTS * k * WIDTH + 2 * units * n + 26 * b * units + 40 * b * (k + n)
    return b % 16 == 0 and k % 128 == 0 and units % WIDTH == 0 and n % 128 == 0 and held < 57 * 2**20


def solution(mesh):
    specs = dict(
        mesh=mesh,
        in_specs=(P(("groups", "row"), "col"), P("col", "row"), P("col", "row"), P("row", "col")),
        out_specs=P(("groups", "row"), "col"),
        check_vma=False,
    )

    def layer(tokens, gate_weight, up_weight, down_weight):
        body = fused if fits(mesh, tokens, gate_weight, down_weight) else plain
        return jax.shard_map(body, **specs)(tokens, gate_weight, up_weight, down_weight)

    return layer
```

```python
import functools

import jax
import jax.numpy as jnp
from jax import lax
from jax.experimental import pallas as pl
from jax.experimental.pallas import tpu as pltpu
from jax.sharding import PartitionSpec as P

MESH = pl.DeviceIdType.MESH
WIDTH = 256
SLOTS = 11


def swiglu(gate, up):
    return (jax.nn.silu(gate) * up).astype(jnp.bfloat16)


def plain(tokens, gate_weight, up_weight, down_weight):
    local_width = gate_weight.shape[1]
    portion = lax.all_gather(tokens, "row", axis=0, tiled=True)
    gate_part = jnp.dot(portion, gate_weight, preferred_element_type=jnp.float32)
    up_part = jnp.dot(portion, up_weight, preferred_element_type=jnp.float32)
    partials = jnp.concatenate([gate_part, up_part], axis=1)
    summed = lax.psum(partials.astype(jnp.bfloat16), "col").astype(jnp.float32)
    hidden = swiglu(summed[:, :local_width], summed[:, local_width:])
    return lax.psum_scatter(
        jnp.dot(hidden, down_weight, preferred_element_type=jnp.float32).astype(jnp.bfloat16),
        "row",
        scatter_dimension=0,
        tiled=True,
    )


def kernel(
    tok_hbm, gate_hbm, up_hbm, down_hbm, out_ref,
    tok, pair_v, down_v, pown, cs, cr, sown, xs, xr, hid, acc, obuf, zr,
    own_sem, gate_sem, up_sem, down_sem, tz_send, tz_recv,
    c_send, c_recv, x_send, x_recv, hx_send, hx_recv, h0_send, h0_recv, oz_send, oz_recv,
):
    g, r, c = lax.axis_index("groups"), lax.axis_index("row"), lax.axis_index("col")
    x, core = c // 2, c % 2
    core_peer = {"col": x * 2 + (1 - core)}
    x_peer = {"col": (1 - x) * 2 + core}
    b = tok_hbm.shape[0]
    slots = pair_v.shape[0]
    chunks = down_v.shape[0]
    T = 4 * b
    q, h = b, 2 * b

    def place(row):
        return ((row // 2 + core) % 2) * 2 + (row % 2 + x) % 2

    barrier = pltpu.get_barrier_semaphore()
    for peer in [core_peer, x_peer] + [{"row": (r + k) % 4} for k in (1, 2, 3)]:
        pl.semaphore_signal(barrier, inc=1, device_id=peer, device_id_type=MESH)

    own = pltpu.make_async_copy(tok_hbm, tok.at[place(r)], own_sem)
    own.start()

    def gate_copy(i):
        at = pl.ds(pl.multiple_of(i * WIDTH, WIDTH), WIDTH)
        return pltpu.make_async_copy(gate_hbm.at[:, at], pair_v.at[i % slots, :, pl.ds(0, WIDTH)], gate_sem.at[i % slots])

    def up_copy(i):
        at = pl.ds(pl.multiple_of(i * WIDTH, WIDTH), WIDTH)
        return pltpu.make_async_copy(up_hbm.at[:, at], pair_v.at[i % slots, :, pl.ds(WIDTH, WIDTH)], up_sem.at[i % slots])

    def down_copy(i):
        rows = pl.ds(pl.multiple_of(i * WIDTH, WIDTH), WIDTH)
        return pltpu.make_async_copy(down_hbm.at[rows], down_v.at[i], down_sem.at[i])

    def start_weights(i, carry):
        gate_copy(i).start()
        up_copy(i).start()
        return carry

    def start_down(i, carry):
        down_copy(i).start()
        return carry

    start_weights(0, 0)
    pl.semaphore_wait(barrier, 5)

    def send(src, dst, send_sem, recv_sem, peer):
        return pltpu.make_async_remote_copy(
            src_ref=src, dst_ref=dst, send_sem=send_sem, recv_sem=recv_sem,
            device_id=peer, device_id_type=MESH,
        )

    def tok_copy(k):
        to = {"row": (r + k) % 4}
        return send(tok_hbm, tok.at[place(r)], tz_send.at[k - 1], tz_recv.at[k - 1], to)

    def tok_in(k):
        block = tok.at[place((r + 4 - k) % 4)]
        return send(block, block, tz_send.at[k - 1], tz_recv.at[k - 1], {"row": (r + k) % 4})

    for k in (2, 1, 3):
        tok_copy(k).start()
    lax.fori_loop(1, slots, start_weights, 0)
    acc[...] = jnp.zeros_like(acc)
    own.wait()
    for k in (1, 3, 2):
        tok_in(k).wait_recv()

    def c_copy(i):
        return send(cs.at[i], cr.at[i], c_send.at[i], c_recv.at[i], core_peer)

    def x_copy(i):
        return send(xs.at[i], xr.at[i], x_send.at[i], x_recv.at[i], x_peer)

    def hx_copy(i):
        return send(hid.at[i, pl.ds(0, q)], hid.at[i, pl.ds(q, q)], hx_send.at[i], hx_recv.at[i], x_peer)

    def h0_copy(i):
        return send(hid.at[i, pl.ds(0, h)], hid.at[i, pl.ds(h, h)], h0_send.at[i], h0_recv.at[i], core_peer)

    def project(i):
        gate_copy(i).wait()
        up_copy(i).wait()
        t = tok[...].reshape(T, tok.shape[2])
        p = jnp.dot(t, pair_v[i % slots], preferred_element_type=jnp.float32)
        pown[i] = p[:h]
        cs[i] = p[h:].astype(jnp.bfloat16)
        c_copy(i).start()

        @pl.when(i + slots < chunks)
        def _():
            start_weights(i + slots, 0)

        @pl.when(i == max(chunks - slots - 1, 0))
        def _():
            lax.fori_loop(0, chunks, start_down, 0)

    def add_core(i):
        c_copy(i).wait_recv()
        s = pown[i] + cr[i].astype(jnp.float32)
        sown[i] = s[:q]
        xs[i] = s[q:].astype(jnp.bfloat16)
        x_copy(i).start()

    def add_x(i):
        x_copy(i).wait_recv()
        s = sown[i] + xr[i].astype(jnp.float32)
        gate, up = s[:, :WIDTH], s[:, WIDTH:]
        hid[i, pl.ds(0, q), :] = (gate / (1.0 + jnp.exp(-gate)) * up).astype(jnp.bfloat16)
        hx_copy(i).start()

    def spread(i):
        hx_copy(i).wait_recv()
        h0_copy(i).start()

    def contract(i):
        down_copy(i).wait()
        h0_copy(i).wait_recv()

        @pl.when(i % 2 == 1)
        def _():
            first = pl.ds(i - 1, 2)
            two = jnp.concatenate([hid[i - 1], hid[i]], axis=1)
            acc[...] += jnp.dot(two, down_v[first].reshape(2 * WIDTH, down_v.shape[2]), preferred_element_type=jnp.float32)

    stages = ((spread, 24), (add_x, 14), (add_core, 4), (project, 0), (contract, 26))

    def step(t, carry):
        for stage, lag in stages:
            i = t - lag
            pl.when(jnp.logical_and(i >= 0, i < chunks))(functools.partial(stage, i))
        return carry

    lax.fori_loop(0, chunks + 26, step, 0)

    def out_copy(k):
        row = (r + k) % 4
        return send(obuf.at[place(row)], zr.at[k - 1], oz_send.at[k - 1], oz_recv.at[k - 1], {"row": row})

    obuf[...] = acc[...].astype(jnp.bfloat16).reshape(obuf.shape)
    for k in (2, 1, 3):
        out_copy(k).start()

    def drain(i, carry):
        for copy in (c_copy, x_copy, hx_copy, h0_copy):
            copy(i).wait_send()
        return carry

    lax.fori_loop(0, chunks, drain, 0)
    for k in (1, 2, 3):
        tok_copy(k).wait_send()
    total = acc[pl.ds(pl.multiple_of(place(r) * b, b), b), :]
    for k in (1, 3, 2):
        out_copy(k).wait_recv()
        total = total + zr[k - 1].astype(jnp.float32)
    out_ref[...] = total.astype(jnp.bfloat16)
    for k in (1, 2, 3):
        out_copy(k).wait_send()


def fused(tokens, gate_weight, up_weight, down_weight):
    b, k = tokens.shape
    units = gate_weight.shape[1]
    n = down_weight.shape[1]
    chunks = units // WIDTH
    slots = min(SLOTS, chunks)
    T = 4 * b
    q, h = b, 2 * b
    bf16, f32 = jnp.bfloat16, jnp.float32
    dma = pltpu.SemaphoreType.DMA
    per_chunk = dma((chunks,))
    return pl.pallas_call(
        kernel,
        out_shape=jax.ShapeDtypeStruct((b, n), bf16),
        in_specs=[pl.BlockSpec(memory_space=pl.ANY)] * 4,
        out_specs=pl.BlockSpec(memory_space=pltpu.VMEM),
        scratch_shapes=[
            pltpu.VMEM((4, b, k), bf16),
            pltpu.VMEM((slots, k, 2 * WIDTH), bf16),
            pltpu.VMEM((chunks, WIDTH, n), bf16),
            pltpu.VMEM((chunks, h, 2 * WIDTH), f32),
            pltpu.VMEM((chunks, h, 2 * WIDTH), bf16),
            pltpu.VMEM((chunks, h, 2 * WIDTH), bf16),
            pltpu.VMEM((chunks, q, 2 * WIDTH), f32),
            pltpu.VMEM((chunks, q, 2 * WIDTH), bf16),
            pltpu.VMEM((chunks, q, 2 * WIDTH), bf16),
            pltpu.VMEM((chunks, T, WIDTH), bf16),
            pltpu.VMEM((T, n), f32),
            pltpu.VMEM((4, b, n), bf16),
            pltpu.VMEM((3, b, n), bf16),
            dma,
            dma((slots,)),
            dma((slots,)),
            per_chunk,
            dma((3,)),
            dma((3,)),
        ]
        + [per_chunk] * 8
        + [dma((3,)), dma((3,))],
        compiler_params=pltpu.CompilerParams(
            collective_id=0, has_side_effects=True, vmem_limit_bytes=60 * 2**20
        ),
        cost_estimate=pl.CostEstimate(
            flops=6 * T * k * units, bytes_accessed=6 * k * units, transcendentals=q * units
        ),
    )(tokens, gate_weight, up_weight, down_weight)


def fits(mesh, tokens, gate_weight, down_weight):
    s = mesh.shape
    if (s["groups"], s["row"], s["col"]) != (2, 4, 4):
        return False
    b, k = tokens.shape[0] // 8, tokens.shape[1] // 4
    units, n = gate_weight.shape[1] // 4, down_weight.shape[1] // 4
    held = 4 * SLOTS * k * WIDTH + 2 * units * n + 26 * b * units + 40 * b * (k + n)
    return b % 16 == 0 and k % 128 == 0 and units % (2 * WIDTH) == 0 and n % 128 == 0 and held < 57 * 2**20


def solution(mesh):
    specs = dict(
        mesh=mesh,
        in_specs=(P(("groups", "row"), "col"), P("col", "row"), P("col", "row"), P("row", "col")),
        out_specs=P(("groups", "row"), "col"),
        check_vma=False,
    )

    def layer(tokens, gate_weight, up_weight, down_weight):
        body = fused if fits(mesh, tokens, gate_weight, down_weight) else plain
        return jax.shard_map(body, **specs)(tokens, gate_weight, up_weight, down_weight)

    return layer
```
